128 devices in a mesh: dp: 32 (over x, z, core), mp: 4 (over y).
Axes of the slice: x: 4, y: 4, z: 4, core: 2. Of those that a mesh axis runs over, the one named last changes fastest.
Arguments:
- attn_out: bfloat16 [32768, 3072], P('dp', 'mp'), may hold values from -80 to 80
- cotangent: bfloat16 [32768, 6144], P('dp'), may hold values from -60 to 60
- master_weight: float32 [3072, 6144], P(('mp', 'dp')), may hold values from -0.1 to 0.1
- moment_weight: float32 [3072, 6144], P(('mp', 'dp')), may hold values from -0.1 to 0.1
- second_weight: float32 [3072, 6144], P(('mp', 'dp')), may hold values from 0.01 to 1
- teacher_weight: float32 [3072, 6144], P(('mp', 'dp')), may hold values from -0.1 to 0.1
- master_bias: float32 [6144], P('dp'), may hold values from -0.1 to 0.1
- moment_bias: float32 [6144], P('dp'), may hold values from -0.1 to 0.1
- second_bias: float32 [6144], P('dp'), may hold values from 0.01 to 1
- teacher_bias: float32 [6144], P('dp'), may hold values from -0.1 to 0.1
Outputs:
- new_master_weight: float32 [3072, 6144], P(('mp', 'dp'))
- new_moment_weight: float32 [3072, 6144], P(('mp', 'dp'))
- new_second_weight: float32 [3072, 6144], P(('mp', 'dp'))
- new_teacher_weight: float32 [3072, 6144], P(('mp', 'dp'))
- new_master_bias: float32 [6144], P('dp')
- new_moment_bias: float32 [6144], P('dp')
- new_second_bias: float32 [6144], P('dp')
- new_teacher_bias: float32 [6144], P('dp')
- teacher_weight_full: bfloat16 [3072, 6144], P('mp')
- teacher_bias_full: bfloat16 [6144], replicated
The draws below stay inside these ranges and needn't reach their ends.
All inputs are finite; a program needn't handle non-finite values.
Results may differ from the reference program's by a relative error of at most 0.00045.
Values may be sent and summed in bfloat16 or wider, within the bound.
No kernel may reach another device: no remote copies, remote signals or barrier semaphores. Data moves between devices by JAX's collectives and lax.ppermute only.
A program may use at most 128 MiB of HBM per device.

```python
import math
import jax
import jax.numpy as jnp
from jax import lax

D = 6144
TOK_DEV = 1024
HW = 3072
TOKENS = 32768
N_DP = 32


def draw_attn_out(key, part):
    key_base = jax.random.fold_in(key, 11)
    key_rough = jax.random.fold_in(key, 12)
    column_pos = jnp.arange(HW).astype(jnp.float32)
    roughness = jnp.exp(jax.random.uniform(key_rough, (HW,), jnp.float32, -0.5, 0.5))
    level = 0.167 * jnp.sqrt(jnp.float32(TOKENS) / jnp.float32(HW))
    scales = level * 10.0 ** (2.0 * column_pos / HW - 1.0) * roughness
    values = scales * jax.random.truncated_normal(key_base, -4.0, 4.0, (TOKENS, HW), jnp.float32)
    return values.astype(jnp.bfloat16)


def draw_cotangent(key, part):
    key_base = jax.random.fold_in(key, 21)
    key_scale = jax.random.fold_in(key, 22)
    key_sign = jax.random.fold_in(key, 24)
    scales = jnp.exp(jax.random.uniform(key_scale, (D,), jnp.float32, 0.0, 2.302585))
    column_pos = jnp.arange(D).astype(jnp.float32)
    signs = 2.0 * jax.random.bernoulli(key_sign, 0.5, (D,)).astype(jnp.float32) - 1.0
    offsets = signs * (0.25 + 0.75 * column_pos / D)
    values = scales * (jax.random.truncated_normal(key_base, -4.0, 4.0, (TOKENS, D), jnp.float32) + offsets)
    return values.astype(jnp.bfloat16)


def steps_of(key, dims, pieces, smallest, largest):
    def one(axis_at, parts):
        steps = jax.random.uniform(jax.random.fold_in(jax.random.fold_in(key, 6), axis_at), (parts,), jnp.float32, smallest / len(pieces), largest / len(pieces))
        return jnp.repeat(jnp.exp(steps), dims[axis_at] // parts).reshape((-1,) + (1,) * (len(dims) - axis_at - 1))

    gain = one(*pieces[0])
    for cut in pieces[1:]:
        gain = gain * one(*cut)
    return gain


def normal_values(stream_key, shape, scale, reach, pieces=(), kind=jnp.bfloat16):
    gain = steps_of(stream_key, shape, pieces, -0.22, 0.18) if pieces else 1.0
    result = jax.random.normal(stream_key, shape, jnp.float32) * scale * gain
    return jnp.minimum(jnp.maximum(result, -reach), reach).astype(kind)


def setup_inputs(seed: int = 0) -> dict:
    keys = jax.random.split(jax.random.key(seed), 11)
    attn_out = draw_attn_out(jax.random.fold_in(keys[10], 71), 0)
    cotangent = draw_cotangent(jax.random.fold_in(keys[10], 71), 0)
    master_weight = normal_values(keys[2], (HW, D), 0.02, 0.1, ((0, 128),), jnp.float32)
    moment_weight = normal_values(keys[3], (HW, D), 0.03, 0.1, ((0, 128),), jnp.float32)
    second_weight = jnp.clip(jnp.exp(math.log(1.0) - 4.6051702 * jax.random.uniform(keys[4], (HW, D), jnp.float32) ** steps_of(keys[4], (HW, D), ((0, 128),), -0.2, 0.2)), 0.01, 1.0)
    teacher_weight = normal_values(keys[5], (HW, D), 0.02, 0.1, ((0, 128),), jnp.float32)
    master_bias = normal_values(keys[6], (D,), 0.02, 0.1, ((0, 32),), jnp.float32)
    moment_bias = normal_values(keys[7], (D,), 0.03, 0.1, ((0, 32),), jnp.float32)
    second_bias = jnp.clip(jnp.exp(math.log(1.0) - 4.6051702 * jax.random.uniform(keys[8], (D,), jnp.float32) ** steps_of(keys[8], (D,), ((0, 32),), -0.2, 0.2)), 0.01, 1.0)
    teacher_bias = normal_values(keys[9], (D,), 0.02, 0.1, ((0, 32),), jnp.float32)
    return dict(attn_out=attn_out, cotangent=cotangent, master_weight=master_weight, moment_weight=moment_weight, second_weight=second_weight, teacher_weight=teacher_weight, master_bias=master_bias, moment_bias=moment_bias, second_bias=second_bias, teacher_bias=teacher_bias)


beta_one = 0.9
beta_two = 0.95
adam_eps = 1e-08
learn_rate = 0.1
decay_rate = 0.05
ema_keep = 0.9

def adamw_update(gradient, master, moment, second, teacher, clip_factor, decay):
    clipped = clip_factor * gradient
    new_moment = beta_one * moment + (1.0 - beta_one) * clipped
    new_second = beta_two * second + (1.0 - beta_two) * clipped * clipped
    new_master = master - learn_rate * (new_moment / (jnp.sqrt(new_second) + adam_eps) + decay * master)
    new_teacher = ema_keep * teacher + (1.0 - ema_keep) * new_master
    return (new_master, new_moment, new_second, new_teacher)

def reference(attn_out, cotangent, master_weight, moment_weight, second_weight, teacher_weight, master_bias, moment_bias, second_bias, teacher_bias):
    blocks_in = attn_out.reshape(N_DP, TOK_DEV, HW)
    blocks_out = cotangent.reshape(N_DP, TOK_DEV, D)

    def accumulate(total, pair):
        partial_grad = jnp.dot(pair[0].T, pair[1], preferred_element_type=jnp.float32)
        return (total + partial_grad, None)
    weight_grad, unused_out = lax.scan(accumulate, jnp.zeros((HW, D), jnp.float32), (blocks_in, blocks_out))
    bias_grad = lax.optimization_barrier(jnp.sum(cotangent, axis=0, dtype=jnp.float32))
    sq_norm = jnp.sum(weight_grad * weight_grad) + jnp.sum(bias_grad * bias_grad)
    clip_factor = jnp.minimum(1.0, jnp.sqrt(jnp.float32(HW * D + D)) / jnp.sqrt(sq_norm + 1e-06))
    master_w, moment_w, second_w, teacher_w = adamw_update(weight_grad, master_weight, moment_weight, second_weight, teacher_weight, clip_factor, decay_rate)
    master_b, moment_b, second_b, teacher_b = adamw_update(bias_grad, master_bias, moment_bias, second_bias, teacher_bias, clip_factor, 0.0)
    return (master_w, moment_w, second_w, teacher_w, master_b, moment_b, second_b, teacher_b, teacher_w.astype(jnp.bfloat16), teacher_b.astype(jnp.bfloat16))
```

```python
import jax
import jax.numpy as jnp
from jax import lax
from jax.sharding import PartitionSpec as P

beta_one = 0.9
beta_two = 0.95
adam_eps = 1e-08
learn_rate = 0.1
decay_rate = 0.05
ema_keep = 0.9
X, Z, C, Y = 4, 4, 2, 4


def adamw_update(gradient, master, moment, second, teacher, clip_factor, decay):
    clipped = clip_factor * gradient
    new_moment = beta_one * moment + (1.0 - beta_one) * clipped
    new_second = beta_two * second + (1.0 - beta_two) * clipped * clipped
    new_master = master - learn_rate * (
        new_moment / (jnp.sqrt(new_second) + adam_eps) + decay * master
    )
    new_teacher = ema_keep * teacher + (1.0 - ema_keep) * new_master
    return (new_master, new_moment, new_second, new_teacher)


def transposed_product(left, right):
    return lax.dot_general(
        left, right, (((0,), (0,)), ((), ())), preferred_element_type=jnp.float32
    )


def place(x, z, c):
    return (x % X) * (Z * C) + (z % Z) * C + c % C


def shift(array, dx=0, dz=0, dc=0):
    pairs = [
        (place(x, z, c), place(x + dx, z + dz, c + dc))
        for x in range(X)
        for z in range(Z)
        for c in range(C)
    ]
    return lax.ppermute(array, "dp", pairs)


def shift_y(array, dy):
    return lax.ppermute(array, "mp", [(y, (y + dy) % Y) for y in range(Y)])


def along_x(array, d):
    return shift(array, dx=d)


def along_z(array, d):
    return shift(array, dz=d)


def all_sum(array, ways):
    for way in ways:
        if way == "core":
            array = array + shift(array, dc=1)
        else:
            move = {"x": along_x, "z": along_z, "y": shift_y}[way]
            array = array + move(array, 1) + move(array, 2) + move(array, 3)
    return array


def pick(array, axis, index):
    return lax.dynamic_index_in_dim(array, index % array.shape[axis], axis, keepdims=False)


def scatter_sum(blocks, axis, me, move):
    total = pick(blocks, axis, me)
    for d in (2, 1, 3):
        total = total + move(pick(blocks, axis, me + d), d)
    return total


def reduce_x_first(product, x, z):
    rows, cols = product.shape
    blocks = product.reshape(X, Z, rows // (X * Z), cols)
    part = scatter_sum(blocks, 0, x, along_x)
    return scatter_sum(part, 0, z, along_z)


def reduce_z_first(product, x, z):
    rows, cols = product.shape
    blocks = product.reshape(X, Z, rows // (X * Z), cols)
    part = scatter_sum(blocks, 1, z, along_z)
    return scatter_sum(part, 0, x, along_x)


def squares(array):
    rows, cols = array.shape
    return jnp.sum((array * array).reshape(rows // 8, 8, cols // 128, 128), axis=(0, 2))


def per_device(
    attn_out,
    cotangent,
    master_weight,
    moment_weight,
    second_weight,
    teacher_weight,
    master_bias,
    moment_bias,
    second_bias,
    teacher_bias,
):
    index = lax.axis_index("dp")
    x, z, c = index // (Z * C), (index // C) % Z, index % C
    width = cotangent.shape[1]
    half, quarter = width // 2, width // 4
    tokens = cotangent.shape[0]
    own_rows = master_weight.shape[0]

    def columns(start):
        return lax.dynamic_slice(cotangent, (0, start), (tokens, quarter))

    attn_other = shift(attn_out, dc=1)
    grads, sums = [], []
    for which, reduce_in in ((0, reduce_x_first), (1, reduce_z_first)):
        other = shift(columns((1 - c) * half + which * quarter), dc=1)
        product = transposed_product(attn_out, columns(c * half + which * quarter))
        product = product + transposed_product(attn_other, other)
        grad = reduce_in(product, x, z)
        grads.append(grad)
        sums.append(squares(grad))
    chip_grad = jnp.concatenate(grads, axis=1).reshape(C, own_rows, half)
    own_half = pick(chip_grad, 0, c)
    other_half = shift(pick(chip_grad, 0, 1 - c), dc=1)
    first = jnp.where(c == 0, own_half, other_half)
    last = jnp.where(c == 0, other_half, own_half)
    weight_grad = jnp.concatenate([first, last], axis=1)

    bias_term = jnp.sum(cotangent, axis=0, dtype=jnp.float32)
    state = jnp.stack([master_bias, moment_bias, second_bias, teacher_bias])
    spread = lax.dynamic_update_slice(
        jnp.zeros((4, width), jnp.float32), state, (0, index * master_bias.shape[0])
    )
    packed = jnp.concatenate([bias_term.reshape(-1, 128), spread.reshape(-1, 128)], axis=0)
    packed = all_sum(packed, ("core", "x", "z")).reshape(5, width)
    bias_grad, bias_state = packed[0], packed[1:]

    sq_norm = jnp.sum(all_sum(sums[0] + sums[1], ("core", "x", "z", "y")))
    sq_norm = sq_norm + jnp.sum(bias_grad * bias_grad)
    total_count = width * (own_rows * X * Z * C * Y + 1)
    clip_factor = jnp.minimum(1.0, jnp.sqrt(jnp.float32(total_count)) / jnp.sqrt(sq_norm + 1e-06))
    master_w, moment_w, second_w, teacher_w = adamw_update(
        weight_grad,
        master_weight,
        moment_weight,
        second_weight,
        teacher_weight,
        clip_factor,
        decay_rate,
    )
    bias_new = adamw_update(bias_grad, *bias_state, clip_factor, 0.0)
    count = master_bias.shape[0]
    own_bias = [lax.dynamic_slice(b, (index * count,), (count,)) for b in bias_new]
    full_bias = bias_new[3].astype(jnp.bfloat16)
    full_weight = lax.all_gather(teacher_w.astype(jnp.bfloat16), "dp", axis=0, tiled=True)
    return (master_w, moment_w, second_w, teacher_w, *own_bias, full_weight, full_bias)


def solution(mesh):
    placed = (
        P("dp", "mp"),
        P("dp", None),
        P(("mp", "dp"), None),
        P(("mp", "dp"), None),
        P(("mp", "dp"), None),
        P(("mp", "dp"), None),
        P("dp"),
        P("dp"),
        P("dp"),
        P("dp"),
    )
    return jax.shard_map(
        per_device,
        mesh=mesh,
        in_specs=placed,
        out_specs=(
            P(("mp", "dp"), None),
            P(("mp", "dp"), None),
            P(("mp", "dp"), None),
            P(("mp", "dp"), None),
            P("dp"),
            P("dp"),
            P("dp"),
            P("dp"),
            P("mp", None),
            P(),
        ),
        check_vma=False,
    )
```

```python
import functools
import jax
import jax.numpy as jnp
from jax import lax
from jax.experimental import pallas as pl
from jax.experimental.pallas import tpu as pltpu
from jax.sharding import PartitionSpec as P

beta_one = 0.9
beta_two = 0.95
adam_eps = 1e-08
learn_rate = 0.1
decay_rate = 0.05
ema_keep = 0.9
X, Z, C, Y = 4, 4, 2, 4


def adamw_update(gradient, master, moment, second, teacher, clip_factor, decay):
    clipped = clip_factor * gradient
    new_moment = beta_one * moment + (1.0 - beta_one) * clipped
    new_second = beta_two * second + (1.0 - beta_two) * clipped * clipped
    new_master = master - learn_rate * (
        new_moment / (jnp.sqrt(new_second) + adam_eps) + decay * master
    )
    new_teacher = ema_keep * teacher + (1.0 - ema_keep) * new_master
    return (new_master, new_moment, new_second, new_teacher)


NOTE = 8


def product_kernel(x_first, side, own, other, own_cols, other_cols, out):
    dims = (((0,), (0,)), ((), ()))
    value = lax.dot_general(own[...], own_cols[...], dims, preferred_element_type=jnp.float32)
    value += lax.dot_general(other[...], other_cols[...], dims, preferred_element_type=jnp.float32)
    peak = jnp.max(jnp.abs(value), axis=0, keepdims=True)
    power = jnp.ceil(jnp.log2(jnp.maximum(peak, 1e-30))) + 1.0
    value = value * jnp.exp2(15.0 - power)
    rows, cols = value.shape
    block = rows // X
    small = block // Z
    for i in range(X):
        if x_first:
            out[i, :block, :] = value[i * block : (i + 1) * block]
        else:
            for j in range(X):
                at = j * block + i * small
                out[i, j * small : (j + 1) * small, :] = value[at : at + small]
        out[i, block:, :] = jnp.broadcast_to(power, (NOTE, cols))


def chip_product(attn_own, attn_other, cotangent, start, other_cols, x_first):
    tokens, rows = attn_own.shape
    cols = other_cols.shape[1]
    step = 512
    whole = pl.BlockSpec((tokens, rows), lambda n, side: (0, 0))
    shape = (X, rows // X + NOTE, cols)
    return pl.pallas_call(
        functools.partial(product_kernel, x_first),
        grid_spec=pltpu.PrefetchScalarGridSpec(
            num_scalar_prefetch=1,
            grid=(cols // step,),
            in_specs=[
                whole,
                whole,
                pl.BlockSpec((tokens, step), lambda n, side: (0, side[0] + n)),
                pl.BlockSpec((tokens, step), lambda n, side: (0, n)),
            ],
            out_specs=pl.BlockSpec((*shape[:2], step), lambda n, side: (0, 0, n)),
        ),
        out_shape=jax.ShapeDtypeStruct(shape, jnp.float32),
        compiler_params=pltpu.CompilerParams(
            dimension_semantics=("arbitrary",), vmem_limit_bytes=40 * 2**20
        ),
        cost_estimate=pl.CostEstimate(flops=1, bytes_accessed=1, transcendentals=0),
    )((start // step).reshape(1).astype(jnp.int32), attn_own, attn_other, cotangent, other_cols)


def place(x, z, c):
    return (x % X) * (Z * C) + (z % Z) * C + c % C


def shift(array, dx=0, dz=0, dc=0):
    pairs = [
        (place(x, z, c), place(x + dx, z + dz, c + dc))
        for x in range(X)
        for z in range(Z)
        for c in range(C)
    ]
    return lax.ppermute(array, "dp", pairs)


def shift_y(array, dy):
    return lax.ppermute(array, "mp", [(y, (y + dy) % Y) for y in range(Y)])


def along_x(array, d):
    return shift(array, dx=d)


def along_z(array, d):
    return shift(array, dz=d)


def all_sum(array, ways):
    for way in ways:
        if way == "core":
            array = array + shift(array, dc=1)
        else:
            move = {"x": along_x, "z": along_z, "y": shift_y}[way]
            array = array + move(array, 1) + move(array, 2) + move(array, 3)
    return array


def pick(array, axis, index):
    return lax.dynamic_index_in_dim(array, index % array.shape[axis], axis, keepdims=False)


def scatter_sum(blocks, axis, me, move):
    total = pick(blocks, axis, me)
    for d in (2, 1, 3):
        total = total + move(pick(blocks, axis, me + d), d)
    return total


def coded_pieces(blocks, me):
    return [pick(blocks, 0, me + d).astype(jnp.float16) for d in (2, 1, 3)]


def decoded(piece):
    piece = piece.astype(jnp.float32)
    rows = piece.shape[0] - NOTE
    return piece[:rows] * jnp.exp2(piece[rows : rows + 1] - 15.0)


def coded_sum(blocks, pieces, me, move):
    total = decoded(pick(blocks, 0, me))
    for d, piece in zip((2, 1, 3), pieces):
        total = total + decoded(move(piece, d))
    return total.reshape(X, -1, total.shape[1])


def gather_line(own, me, move):
    got = [own] + [move(own, d) for d in (1, 2, 3)]
    turned = jnp.stack([got[3], got[2], got[1], got[0], got[3], got[2], got[1]])
    return lax.dynamic_slice_in_dim(turned, 3 - me, 4, axis=0)


def nothing(out):
    pass


def blank(shape, dtype):
    return pl.pallas_call(
        nothing,
        out_shape=jax.ShapeDtypeStruct(shape, dtype),
        out_specs=pl.BlockSpec(memory_space=pl.ANY),
    )()


def gather_plane(rows, x, z, c):
    count, width = rows.shape
    half = width // 2
    full = blank((X, Z, C, count, width), rows.dtype)
    lines = [gather_line(rows[:, :half], z, along_z), gather_line(rows[:, half:], x, along_x)]
    lines = lax.optimization_barrier(lines)
    moves = (along_x, along_z)
    near = [(which, d, moves[which](lines[which], d)) for d in (1, -1) for which in (0, 1)]
    far = []
    for which, d, line in near:
        low = 0 if d == 1 else 2
        far.append((which, 2, low, moves[which](line[low : low + 2], d)))
    parts = [(which, 0, 0, lines[which]) for which in (0, 1)]
    parts += [(which, d, 0, line) for which, d, line in near]
    for which, d, low, part in parts + far:
        zero, start = jnp.int32(0), jnp.int32(which * half)
        for side, piece in ((c, part), (1 - c, shift(part, dc=1))):
            if which == 0:
                piece, at = piece[None, :, None], ((x - d) % X, jnp.int32(low))
            else:
                piece, at = piece[:, None, None], (jnp.int32(low), (z - d) % Z)
            full = lax.dynamic_update_slice(full, piece, (*at, side, zero, start))
    return full.reshape(X * Z * C * count, width)


def squares(array):
    rows, cols = array.shape
    return jnp.sum((array * array).reshape(rows // 8, 8, cols // 128, 128), axis=(0, 2))


def per_device(
    attn_out,
    cotangent,
    master_weight,
    moment_weight,
    second_weight,
    teacher_weight,
    master_bias,
    moment_bias,
    second_bias,
    teacher_bias,
):
    index = lax.axis_index("dp")
    x, z, c = index // (Z * C), (index // C) % Z, index % C
    width = cotangent.shape[1]
    half, quarter = width // 2, width // 4
    tokens = cotangent.shape[0]
    own_rows = master_weight.shape[0]

    def columns(start):
        return lax.dynamic_slice(cotangent, (0, start), (tokens, quarter))

    attn_other = shift(attn_out, dc=1)
    sent = [columns((1 - c) * half)]
    held, sent[0] = lax.optimization_barrier((cotangent, sent[0]))
    sent.append(lax.dynamic_slice(held, (0, (1 - c) * half + quarter), (tokens, quarter)))
    others = [shift(part, dc=1) for part in sent]
    bias_term = jnp.sum(held, axis=0, dtype=jnp.float32)

    others[0], bias_term = lax.optimization_barrier((others[0], bias_term))

    def blocks_of(which):
        start = c * half + which * quarter
        return chip_product(attn_out, attn_other, cotangent, start, others[which], which == 0)

    blocks_a = blocks_of(0)
    pieces_a = coded_pieces(blocks_a, x)
    others[1], pieces_a = lax.optimization_barrier((others[1], pieces_a))
    blocks_b = blocks_of(1)
    pieces_b = coded_pieces(blocks_b, z)
    part_a = coded_sum(blocks_a, pieces_a, x, along_x)
    part_b = coded_sum(blocks_b, pieces_b, z, along_z)
    grads = [scatter_sum(part_a, 0, z, along_z), scatter_sum(part_b, 0, x, along_x)]
    sums = [squares(g) for g in grads]
    chip_grad = jnp.concatenate(grads, axis=1).reshape(C, own_rows, half)
    own_half = pick(chip_grad, 0, c)
    other_half = shift(pick(chip_grad, 0, 1 - c), dc=1)
    first = jnp.where(c == 0, own_half, other_half)
    last = jnp.where(c == 0, other_half, own_half)
    weight_grad = jnp.concatenate([first, last], axis=1)

    count = master_bias.shape[0]
    state = jnp.stack([master_bias, moment_bias, second_bias, teacher_bias])
    spread = lax.dynamic_update_slice(jnp.zeros((4, width), jnp.float32), state, (0, index * count))
    packed = jnp.concatenate([bias_term.reshape(-1, 128), spread.reshape(-1, 128)], axis=0)
    packed = all_sum(packed, ("core", "x", "z")).reshape(5, width)
    bias_grad, bias_state = packed[0], packed[1:]

    sq_norm = jnp.sum(all_sum(sums[0] + sums[1], ("core", "x", "z", "y")))
    sq_norm = sq_norm + jnp.sum(bias_grad * bias_grad)
    total_count = width * (own_rows * X * Z * C * Y + 1)
    clip_factor = jnp.minimum(1.0, jnp.sqrt(jnp.float32(total_count)) / jnp.sqrt(sq_norm + 1e-06))
    master_w, moment_w, second_w, teacher_w = adamw_update(
        weight_grad,
        master_weight,
        moment_weight,
        second_weight,
        teacher_weight,
        clip_factor,
        decay_rate,
    )
    bias_new = adamw_update(bias_grad, *bias_state, clip_factor, 0.0)
    own_bias = [lax.dynamic_slice(b, (index * count,), (count,)) for b in bias_new]
    full_bias = bias_new[3].astype(jnp.bfloat16)
    full_weight = gather_plane(teacher_w.astype(jnp.bfloat16), x, z, c)
    return (master_w, moment_w, second_w, teacher_w, *own_bias, full_weight, full_bias)


def solution(mesh):
    placed = (
        P("dp", "mp"),
        P("dp", None),
        P(("mp", "dp"), None),
        P(("mp", "dp"), None),
        P(("mp", "dp"), None),
        P(("mp", "dp"), None),
        P("dp"),
        P("dp"),
        P("dp"),
        P("dp"),
    )
    return jax.shard_map(
        per_device,
        mesh=mesh,
        in_specs=placed,
        out_specs=(
            P(("mp", "dp"), None),
            P(("mp", "dp"), None),
            P(("mp", "dp"), None),
            P(("mp", "dp"), None),
            P("dp"),
            P("dp"),
            P("dp"),
            P("dp"),
            P("mp", None),
            P(),
        ),
        check_vma=False,
    )
```

```python
import functools
import jax
import jax.numpy as jnp
from jax import lax
from jax.experimental import pallas as pl
from jax.experimental.pallas import tpu as pltpu
from jax.sharding import PartitionSpec as P

beta_one = 0.9
beta_two = 0.95
adam_eps = 1e-08
learn_rate = 0.1
decay_rate = 0.05
ema_keep = 0.9
X, Z, C, Y = 4, 4, 2, 4


def adamw_update(gradient, master, moment, second, teacher, clip_factor, decay):
    clipped = clip_factor * gradient
    new_moment = beta_one * moment + (1.0 - beta_one) * clipped
    new_second = beta_two * second + (1.0 - beta_two) * clipped * clipped
    new_master = master - learn_rate * (
        new_moment / (jnp.sqrt(new_second) + adam_eps) + decay * master
    )
    new_teacher = ema_keep * teacher + (1.0 - ema_keep) * new_master
    return (new_master, new_moment, new_second, new_teacher)


NOTE = 8
STATE_SCALE = 2.0**14


def product_kernel(x_first, side, own, other, own_cols, other_cols, extra, out):
    dims = (((0,), (0,)), ((), ()))
    value = lax.dot_general(own[...], own_cols[...], dims, preferred_element_type=jnp.float32)
    value += lax.dot_general(other[...], other_cols[...], dims, preferred_element_type=jnp.float32)
    peak = jnp.max(jnp.abs(value), axis=0, keepdims=True)
    power = jnp.ceil(jnp.log2(jnp.maximum(peak, 1e-30))) + 1.0
    value = value * jnp.exp2(15.0 - power)
    rows, cols = value.shape
    bias = sum(jnp.sum(r[...].astype(jnp.float32), axis=0, keepdims=True) for r in (own_cols, other_cols))
    bias_power = jnp.ceil(jnp.log2(jnp.maximum(jnp.abs(bias), 1e-30))) + 1.0
    rest = bias * jnp.exp2(15.0 - bias_power)
    lines = [power]
    for _ in range(2):
        piece = rest.astype(jnp.bfloat16).astype(jnp.float32)
        lines.append(piece)
        rest = rest - piece
    lines += [rest, bias_power]
    row = lax.broadcasted_iota(jnp.int32, (NOTE, cols), 0)
    note = extra[...]
    for at, line in enumerate(lines):
        note = jnp.where(row == at, line, note)
    block = rows // X
    small = block // Z
    for i in range(X):
        if x_first:
            out[i, :block, :] = value[i * block : (i + 1) * block]
        else:
            for j in range(X):
                at = j * block + i * small
                out[i, j * small : (j + 1) * small, :] = value[at : at + small]
        out[i, block:, :] = note


def chip_product(attn_own, attn_other, cotangent, start, other_cols, extra, x_first):
    tokens, rows = attn_own.shape
    cols = other_cols.shape[1]
    step = 512
    whole = pl.BlockSpec((tokens, rows), lambda n, side: (0, 0))
    shape = (X, rows // X + NOTE, cols)
    return pl.pallas_call(
        functools.partial(product_kernel, x_first),
        grid_spec=pltpu.PrefetchScalarGridSpec(
            num_scalar_prefetch=1,
            grid=(cols // step,),
            in_specs=[
                whole,
                whole,
                pl.BlockSpec((tokens, step), lambda n, side: (0, side[0] + n)),
                pl.BlockSpec((tokens, step), lambda n, side: (0, n)),
                pl.BlockSpec((NOTE, step), lambda n, side: (0, n)),
            ],
            out_specs=pl.BlockSpec((*shape[:2], step), lambda n, side: (0, 0, n)),
        ),
        out_shape=jax.ShapeDtypeStruct(shape, jnp.float32),
        compiler_params=pltpu.CompilerParams(
            dimension_semantics=("arbitrary",), vmem_limit_bytes=40 * 2**20
        ),
        cost_estimate=pl.CostEstimate(flops=1, bytes_accessed=1, transcendentals=0),
    )((start // step).reshape(1).astype(jnp.int32), attn_own, attn_other, cotangent, other_cols, extra)


def place(x, z, c):
    return (x % X) * (Z * C) + (z % Z) * C + c % C


def shift(array, dx=0, dz=0, dc=0):
    pairs = [
        (place(x, z, c), place(x + dx, z + dz, c + dc))
        for x in range(X)
        for z in range(Z)
        for c in range(C)
    ]
    return lax.ppermute(array, "dp", pairs)


def shift_y(array, dy):
    return lax.ppermute(array, "mp", [(y, (y + dy) % Y) for y in range(Y)])


def along_x(array, d):
    return shift(array, dx=d)


def along_z(array, d):
    return shift(array, dz=d)


def all_sum(array, ways):
    for way in ways:
        if way == "core":
            array = array + shift(array, dc=1)
        else:
            move = {"x": along_x, "z": along_z, "y": shift_y}[way]
            array = array + move(array, 1) + move(array, 2) + move(array, 3)
    return array


def pick(array, axis, index):
    return lax.dynamic_index_in_dim(array, index % array.shape[axis], axis, keepdims=False)


def turn(array, me, axis):
    back = jnp.flip(array, axis)
    size = array.shape[axis]
    twice = jnp.concatenate([back, lax.slice_in_dim(back, 0, size - 1, axis=axis)], axis=axis)
    return lax.dynamic_slice_in_dim(twice, size - 1 - me, size, axis=axis)


def scatter_sum(blocks, me, rows, move):
    own = pick(blocks, 0, me)
    total, rest = own[:rows], {0: own[rows:]}
    for d in (2, 1, 3):
        got = move(pick(blocks, 0, me + d), d)
        total, rest[d] = total + got[:rows], got[rows:]
    return total, [rest[d] for d in range(4)]


def coded_pieces(blocks, me):
    return [pick(blocks, 0, me + d).astype(jnp.float16) for d in (2, 1, 3)]


def decoded(piece):
    piece = piece.astype(jnp.float32)
    rows = piece.shape[0] - NOTE
    note = [piece[rows + i : rows + i + 1] for i in range(5)]
    value = piece[:rows] * jnp.exp2(note[0] - 15.0)
    return value, (note[1] + note[2] + note[3]) * jnp.exp2(note[4] - 15.0)


def coded_sum(blocks, pieces, me, move, entries):
    own = pick(blocks, 0, me)
    total, bias = decoded(own)
    noted = {0: own[5 - NOTE :, :entries]}
    for d, piece in zip((2, 1, 3), pieces):
        got = move(piece, d)
        value, line = decoded(got)
        total, bias = total + value, bias + line
        noted[d] = got[5 - NOTE :, :entries].astype(jnp.float32)
    cols = total.shape[1]
    lines = [bias]
    if entries:
        lines.append(jnp.stack([jnp.sum(noted[d], axis=0) for d in range(4)]).reshape(-1, cols))
    below = jnp.concatenate(lines, axis=0)
    below = jnp.pad(below, ((0, 8 - below.shape[0]), (0, 0)))
    below = jnp.broadcast_to(below[None], (X, 8, cols))
    return jnp.concatenate([total.reshape(X, -1, cols), below], axis=1)


def gather_line(own, me, move):
    got = [own] + [move(own, d) for d in (1, 2, 3)]
    turned = jnp.stack([got[3], got[2], got[1], got[0], got[3], got[2], got[1]])
    return lax.dynamic_slice_in_dim(turned, 3 - me, 4, axis=0)


def nothing(out):
    pass


def blank(shape, dtype):
    return pl.pallas_call(
        nothing,
        out_shape=jax.ShapeDtypeStruct(shape, dtype),
        out_specs=pl.BlockSpec(memory_space=pl.ANY),
    )()


def by_core(own, twin, axis, c):
    own, twin = jnp.expand_dims(own, axis), jnp.expand_dims(twin, axis)
    shape = [1] * own.ndim
    shape[axis] = C
    return jnp.where(lax.broadcasted_iota(jnp.int32, shape, axis) == c, own, twin)


def gather_plane(rows, x, z, c):
    count, width = rows.shape
    half = width // 2
    full = blank((X, Z, C, count, width), rows.dtype)
    line_a = gather_line(rows[:, :half], z, along_z)
    line_b = gather_line(rows[:, half:], x, along_x)
    line_a, line_b = lax.optimization_barrier((line_a, line_b))
    lines, moves = (line_a, line_b), (along_x, along_z)

    def put(full, which, d, low, part, twin):
        zero, low, start = jnp.int32(0), jnp.int32(low), jnp.int32(which * half)
        piece = by_core(part, twin, 1, c)
        if which == 0:
            piece, at = piece[None], ((x - d) % X, low, zero, zero, start)
        else:
            piece, at = piece[:, None], (low, (z - d) % Z, zero, zero, start)
        return lax.dynamic_update_slice(full, piece, at)

    near = [(i, d, moves[i](lines[i], d)) for d in (1, -1) for i in (0, 1)]
    for i in (0, 1):
        full = put(full, i, 0, 0, lines[i], shift(lines[i], dc=1))
    near_parts, full = lax.optimization_barrier(([part for _, _, part in near], full))
    far = []
    for (i, d, _), part in zip(near, near_parts):
        low = 0 if d == 1 else 2
        far.append((i, low, moves[i](part[low : low + 2], d)))
    for (i, d, _), part in zip(near, near_parts):
        full = put(full, i, d, 0, part, shift(part, dc=1))
    far_parts, full = lax.optimization_barrier(([part for _, _, part in far], full))
    for (i, low, _), part in zip(far, far_parts):
        full = put(full, i, 2, low, part, shift(part, dc=1))
    return full.reshape(X * Z * C * count, width)


def squares(array):
    rows, cols = array.shape
    return jnp.sum((array * array).reshape(rows // 8, 8, cols // 128, 128), axis=(0, 2))


def per_device(
    attn_out,
    cotangent,
    master_weight,
    moment_weight,
    second_weight,
    teacher_weight,
    master_bias,
    moment_bias,
    second_bias,
    teacher_bias,
):
    index = lax.axis_index("dp")
    x, z, c = index // (Z * C), (index // C) % Z, index % C
    width = cotangent.shape[1]
    half, quarter = width // 2, width // 4
    tokens = cotangent.shape[0]
    own_rows = master_weight.shape[0]

    def columns(start):
        return lax.dynamic_slice(cotangent, (0, start), (tokens, quarter))

    attn_other = shift(attn_out, dc=1)
    sent = [columns((1 - c) * half)]
    held, sent[0] = lax.optimization_barrier((cotangent, sent[0]))
    sent.append(lax.dynamic_slice(held, (0, (1 - c) * half + quarter), (tokens, quarter)))
    others = [shift(part, dc=1) for part in sent]
    count = master_bias.shape[0]
    rest = jnp.concatenate([master_bias, moment_bias, second_bias, teacher_bias])[None] * STATE_SCALE
    state = []
    for _ in range(2):
        state.append(lax.reduce_precision(rest, 8, 7))
        rest = rest - state[-1]
    state = jnp.concatenate([*state, rest], axis=0)
    entries = state.shape[1]
    extras = [jnp.pad(state, ((NOTE - 3, 0), (0, quarter - entries))), jnp.zeros((NOTE, quarter), jnp.float32)]

    def blocks_of(which):
        start = c * half + which * quarter
        return chip_product(attn_out, attn_other, cotangent, start, others[which], extras[which], which == 0)

    blocks_a = blocks_of(0)
    pieces_a = coded_pieces(blocks_a, x)
    others[1], pieces_a = lax.optimization_barrier((others[1], pieces_a))
    blocks_b = blocks_of(1)
    pieces_b = coded_pieces(blocks_b, z)
    part_a = coded_sum(blocks_a, pieces_a, x, along_x, entries)
    part_b = coded_sum(blocks_b, pieces_b, z, along_z, 0)
    rows = own_rows * C
    grad_a, noted = scatter_sum(part_a, z, rows + 1, along_z)
    grad_b, _ = scatter_sum(part_b, x, rows + 1, along_x)
    grads = [grad_a, grad_b]
    used = X * entries // quarter
    own_state = jnp.stack([n[:used] for n in noted]).reshape(-1, half)
    sums = [squares(g[:rows]) for g in grads]
    bias_half = jnp.concatenate([g[rows : rows + 1] for g in grads], axis=1)
    chip_grad = jnp.concatenate([g[:rows] for g in grads], axis=1).reshape(C, own_rows, half)
    own_half = pick(chip_grad, 0, c)
    other_half = pick(chip_grad, 0, 1 - c)
    below = jnp.concatenate([bias_half, own_state], axis=0)
    below = jnp.pad(below, ((0, -below.shape[0] % 8), (0, 0)))
    got = shift(jnp.concatenate([other_half, below], axis=0), dc=1)
    other_half, bias_other = got[:own_rows], got[own_rows : own_rows + 1]
    other_state = got[own_rows + 1 : own_rows + 1 + own_state.shape[0]]
    all_state = by_core(*(a.reshape(Z, X, 4, count) for a in (own_state, other_state)), 3, c)
    all_state = turn(turn(all_state, z, 0), x, 1) * (1.0 / STATE_SCALE)
    bias_state = all_state.transpose(2, 1, 0, 3, 4).reshape(4, width)

    def in_order(own, other):
        first, last = jnp.where(c == 0, own, other), jnp.where(c == 0, other, own)
        return jnp.concatenate([first, last], axis=1)

    weight_grad = in_order(own_half, other_half)
    bias_grad = in_order(bias_half, bias_other)[0]

    sq_norm = jnp.sum(all_sum(sums[0] + sums[1], ("core", "x", "z", "y")))
    sq_norm = sq_norm + jnp.sum(bias_grad * bias_grad)
    total_count = width * (own_rows * X * Z * C * Y + 1)
    clip_factor = jnp.minimum(1.0, jnp.sqrt(jnp.float32(total_count)) / jnp.sqrt(sq_norm + 1e-06))
    master_w, moment_w, second_w, teacher_w = adamw_update(
        weight_grad,
        master_weight,
        moment_weight,
        second_weight,
        teacher_weight,
        clip_factor,
        decay_rate,
    )
    own_bias = adamw_update(
        lax.dynamic_slice(bias_grad, (index * count,), (count,)),
        master_bias,
        moment_bias,
        second_bias,
        teacher_bias,
        clip_factor,
        0.0,
    )
    full_bias = adamw_update(bias_grad, *bias_state, clip_factor, 0.0)[3].astype(jnp.bfloat16)
    teacher_half = teacher_w.astype(jnp.bfloat16)
    teacher_half, own_bias, full_bias = lax.optimization_barrier((teacher_half, own_bias, full_bias))
    full_weight = gather_plane(teacher_half, x, z, c)
    return (master_w, moment_w, second_w, teacher_w, *own_bias, full_weight, full_bias)


def solution(mesh):
    placed = (
        P("dp", "mp"),
        P("dp", None),
        P(("mp", "dp"), None),
        P(("mp", "dp"), None),
        P(("mp", "dp"), None),
        P(("mp", "dp"), None),
        P("dp"),
        P("dp"),
        P("dp"),
        P("dp"),
    )
    return jax.shard_map(
        per_device,
        mesh=mesh,
        in_specs=placed,
        out_specs=(
            P(("mp", "dp"), None),
            P(("mp", "dp"), None),
            P(("mp", "dp"), None),
            P(("mp", "dp"), None),
            P("dp"),
            P("dp"),
            P("dp"),
            P("dp"),
            P("mp", None),
            P(),
        ),
        check_vma=False,
    )
```

```python
import functools
import jax
import jax.numpy as jnp
from jax import lax
from jax.experimental import pallas as pl
from jax.experimental.pallas import tpu as pltpu
from jax.sharding import PartitionSpec as P

beta_one = 0.9
beta_two = 0.95
adam_eps = 1e-08
learn_rate = 0.1
decay_rate = 0.05
ema_keep = 0.9
X, Z, C, Y = 4, 4, 2, 4


def adamw_update(gradient, master, moment, second, teacher, clip_factor, decay):
    clipped = clip_factor * gradient
    new_moment = beta_one * moment + (1.0 - beta_one) * clipped
    new_second = beta_two * second + (1.0 - beta_two) * clipped * clipped
    new_master = master - learn_rate * (
        new_moment / (jnp.sqrt(new_second) + adam_eps) + decay * master
    )
    new_teacher = ema_keep * teacher + (1.0 - ema_keep) * new_master
    return (new_master, new_moment, new_second, new_teacher)


NOTE = 8
STATE_SCALE = 2.0**14


def product_kernel(x_first, side, own, other, own_cols, other_cols, extra, out):
    dims = (((0,), (0,)), ((), ()))
    value = lax.dot_general(own[...], own_cols[...], dims, preferred_element_type=jnp.float32)
    value += lax.dot_general(other[...], other_cols[...], dims, preferred_element_type=jnp.float32)
    peak = jnp.max(jnp.abs(value), axis=0, keepdims=True)
    power = jnp.ceil(jnp.log2(jnp.maximum(peak, 1e-30))) + 1.0
    value = value * jnp.exp2(15.0 - power)
    rows, cols = value.shape
    bias = sum(jnp.sum(r[...].astype(jnp.float32), axis=0, keepdims=True) for r in (own_cols, other_cols))
    bias_power = jnp.ceil(jnp.log2(jnp.maximum(jnp.abs(bias), 1e-30))) + 1.0
    rest = bias * jnp.exp2(15.0 - bias_power)
    lines = [power]
    for _ in range(2):
        piece = rest.astype(jnp.bfloat16).astype(jnp.float32)
        lines.append(piece)
        rest = rest - piece
    lines += [rest, bias_power]
    row = lax.broadcasted_iota(jnp.int32, (NOTE, cols), 0)
    note = extra[...]
    for at, line in enumerate(lines):
        note = jnp.where(row == at, line, note)
    block = rows // X
    small = block // Z
    for i in range(X):
        if x_first:
            out[i, :block, :] = value[i * block : (i + 1) * block]
        else:
            for j in range(X):
                at = j * block + i * small
                out[i, j * small : (j + 1) * small, :] = value[at : at + small]
        out[i, block:, :] = note


def chip_product(attn_own, attn_other, cotangent, start, other_cols, extra, x_first):
    tokens, rows = attn_own.shape
    cols = other_cols.shape[1]
    step = 512
    whole = pl.BlockSpec((tokens, rows), lambda n, side: (0, 0))
    shape = (X, rows // X + NOTE, cols)
    return pl.pallas_call(
        functools.partial(product_kernel, x_first),
        grid_spec=pltpu.PrefetchScalarGridSpec(
            num_scalar_prefetch=1,
            grid=(cols // step,),
            in_specs=[
                whole,
                whole,
                pl.BlockSpec((tokens, step), lambda n, side: (0, side[0] + n)),
                pl.BlockSpec((tokens, step), lambda n, side: (0, n)),
                pl.BlockSpec((NOTE, step), lambda n, side: (0, n)),
            ],
            out_specs=pl.BlockSpec((*shape[:2], step), lambda n, side: (0, 0, n)),
        ),
        out_shape=jax.ShapeDtypeStruct(shape, jnp.float32),
        compiler_params=pltpu.CompilerParams(
            dimension_semantics=("arbitrary",), vmem_limit_bytes=40 * 2**20
        ),
        cost_estimate=pl.CostEstimate(flops=1, bytes_accessed=1, transcendentals=0),
    )((start // step).reshape(1).astype(jnp.int32), attn_own, attn_other, cotangent, other_cols, extra)


def place(x, z, c):
    return (x % X) * (Z * C) + (z % Z) * C + c % C


def shift(array, dx=0, dz=0, dc=0):
    pairs = [
        (place(x, z, c), place(x + dx, z + dz, c + dc))
        for x in range(X)
        for z in range(Z)
        for c in range(C)
    ]
    return lax.ppermute(array, "dp", pairs)


def shift_y(array, dy):
    return lax.ppermute(array, "mp", [(y, (y + dy) % Y) for y in range(Y)])


def along_x(array, d):
    return shift(array, dx=d)


def along_z(array, d):
    return shift(array, dz=d)


def all_sum(array, ways):
    for way in ways:
        if way == "core":
            array = array + shift(array, dc=1)
        else:
            move = {"x": along_x, "z": along_z, "y": shift_y}[way]
            array = array + move(array, 1) + move(array, 2) + move(array, 3)
    return array


def pick(array, axis, index):
    return lax.dynamic_index_in_dim(array, index % array.shape[axis], axis, keepdims=False)


def turn(array, me, axis):
    back = jnp.flip(array, axis)
    size = array.shape[axis]
    twice = jnp.concatenate([back, lax.slice_in_dim(back, 0, size - 1, axis=axis)], axis=axis)
    return lax.dynamic_slice_in_dim(twice, size - 1 - me, size, axis=axis)


def scatter_sum(blocks, me, rows, move):
    own = pick(blocks, 0, me)
    total, rest = own[:rows], {0: own[rows:]}
    for d in (2, 1, 3):
        got = move(pick(blocks, 0, me + d), d)
        total, rest[d] = total + got[:rows], got[rows:]
    return total, [rest[d] for d in range(4)]


def coded_pieces(blocks, me):
    return [pick(blocks, 0, me + d).astype(jnp.float16) for d in (2, 1, 3)]


def decoded(piece):
    piece = piece.astype(jnp.float32)
    rows = piece.shape[0] - NOTE
    note = [piece[rows + i : rows + i + 1] for i in range(5)]
    value = piece[:rows] * jnp.exp2(note[0] - 15.0)
    return value, (note[1] + note[2] + note[3]) * jnp.exp2(note[4] - 15.0)


def coded_sum(blocks, pieces, me, move, entries):
    own = pick(blocks, 0, me)
    total, bias = decoded(own)
    noted = {0: own[5 - NOTE :, :entries]}
    for d, piece in zip((2, 1, 3), pieces):
        got = move(piece, d)
        value, line = decoded(got)
        total, bias = total + value, bias + line
        noted[d] = got[5 - NOTE :, :entries].astype(jnp.float32)
    cols = total.shape[1]
    lines = [bias]
    if entries:
        flat = jnp.concatenate([jnp.sum(noted[d], axis=0) for d in range(4)])
        lines.append(jnp.pad(flat, (0, -flat.size % cols)).reshape(-1, cols))
    below = jnp.concatenate(lines, axis=0)
    below = jnp.pad(below, ((0, 8 - below.shape[0]), (0, 0)))
    below = jnp.broadcast_to(below[None], (X, 8, cols))
    return jnp.concatenate([total.reshape(X, -1, cols), below], axis=1)


def gather_line(own, me, move):
    got = [own] + [move(own, d) for d in (1, 2, 3)]
    turned = jnp.stack([got[3], got[2], got[1], got[0], got[3], got[2], got[1]])
    return lax.dynamic_slice_in_dim(turned, 3 - me, 4, axis=0)


def nothing(out):
    pass


def blank(shape, dtype):
    return pl.pallas_call(
        nothing,
        out_shape=jax.ShapeDtypeStruct(shape, dtype),
        out_specs=pl.BlockSpec(memory_space=pl.ANY),
    )()


def by_core(own, twin, axis, c):
    own, twin = jnp.expand_dims(own, axis), jnp.expand_dims(twin, axis)
    shape = [1] * own.ndim
    shape[axis] = C
    return jnp.where(lax.broadcasted_iota(jnp.int32, shape, axis) == c, own, twin)


def gather_plane(rows, x, z, c):
    count, width = rows.shape
    half = width // 2
    full = blank((X, Z, C, count, width), rows.dtype)
    line_a = gather_line(rows[:, :half], z, along_z)
    line_b = gather_line(rows[:, half:], x, along_x)
    line_a, line_b = lax.optimization_barrier((line_a, line_b))
    lines, moves = (line_a, line_b), (along_x, along_z)

    def put(full, which, d, low, part, twin):
        zero, low, start = jnp.int32(0), jnp.int32(low), jnp.int32(which * half)
        piece = by_core(part, twin, 1, c)
        if which == 0:
            piece, at = piece[None], ((x - d) % X, low, zero, zero, start)
        else:
            piece, at = piece[:, None], (low, (z - d) % Z, zero, zero, start)
        return lax.dynamic_update_slice(full, piece, at)

    near = [(i, d, moves[i](lines[i], d)) for d in (1, -1) for i in (0, 1)]
    for i in (0, 1):
        full = put(full, i, 0, 0, lines[i], shift(lines[i], dc=1))
    near_parts, full = lax.optimization_barrier(([part for _, _, part in near], full))
    far = []
    for (i, d, _), part in zip(near, near_parts):
        low = 0 if d == 1 else 2
        far.append((i, low, moves[i](part[low : low + 2], d)))
    twins = lax.optimization_barrier([shift(part, dc=1) for part in near_parts])
    for (i, d, _), part, twin in zip(near, near_parts, twins):
        full = put(full, i, d, 0, part, twin)
    far_parts, full = lax.optimization_barrier(([part for _, _, part in far], full))
    for (i, low, _), part in zip(far, far_parts):
        full = put(full, i, 2, low, part, shift(part, dc=1))
    return full.reshape(X * Z * C * count, width)


def squares(array):
    rows, cols = array.shape
    return jnp.sum((array * array).reshape(rows // 8, 8, cols // 128, 128), axis=(0, 2))


def per_device(
    attn_out,
    cotangent,
    master_weight,
    moment_weight,
    second_weight,
    teacher_weight,
    master_bias,
    moment_bias,
    second_bias,
    teacher_bias,
):
    index = lax.axis_index("dp")
    x, z, c = index // (Z * C), (index // C) % Z, index % C
    width = cotangent.shape[1]
    half = width // 2
    sizes = (half * 1536 // 3072, half * 1536 // 3072)
    tokens = cotangent.shape[0]
    own_rows = master_weight.shape[0]

    def columns(array, which):
        start = (1 - c) * half + which * sizes[0]
        return lax.dynamic_slice(array, (0, start), (tokens, sizes[which]))

    attn_other = shift(attn_out, dc=1)
    sent = [columns(cotangent, 0)]
    held, sent[0] = lax.optimization_barrier((cotangent, sent[0]))
    sent.append(columns(held, 1))
    others = [shift(part, dc=1) for part in sent]
    count = master_bias.shape[0]
    rest = jnp.concatenate([master_bias, moment_bias, second_bias, teacher_bias])[None] * STATE_SCALE
    state = []
    for _ in range(2):
        state.append(lax.reduce_precision(rest, 8, 7))
        rest = rest - state[-1]
    state = jnp.concatenate([*state, rest], axis=0)
    entries = state.shape[1]
    extras = [
        jnp.pad(state, ((NOTE - 3, 0), (0, sizes[0] - entries))),
        jnp.zeros((NOTE, sizes[1]), jnp.float32),
    ]

    def blocks_of(which):
        start = c * half + which * sizes[0]
        return chip_product(attn_out, attn_other, cotangent, start, others[which], extras[which], which == 0)

    blocks_a = blocks_of(0)
    pieces_a = coded_pieces(blocks_a, x)
    others[1], pieces_a = lax.optimization_barrier((others[1], pieces_a))
    blocks_b = blocks_of(1)
    pieces_b = coded_pieces(blocks_b, z)
    part_a = coded_sum(blocks_a, pieces_a, x, along_x, entries)
    part_b = coded_sum(blocks_b, pieces_b, z, along_z, 0)
    rows = own_rows * C
    grad_a, noted = scatter_sum(part_a, z, rows + 1, along_z)
    grad_b, _ = scatter_sum(part_b, x, rows + 1, along_x)
    grads = [grad_a, grad_b]
    own_state = jnp.stack([n.reshape(-1)[: X * entries] for n in noted]).reshape(-1, half)
    sums = [squares(g[:rows]) for g in grads]
    bias_half = jnp.concatenate([g[rows : rows + 1] for g in grads], axis=1)
    chip_grad = jnp.concatenate([g[:rows] for g in grads], axis=1).reshape(C, own_rows, half)
    own_half = pick(chip_grad, 0, c)
    other_half = pick(chip_grad, 0, 1 - c)
    below = jnp.concatenate([bias_half, own_state], axis=0)
    below = jnp.pad(below, ((0, -below.shape[0] % 8), (0, 0)))
    got = shift(jnp.concatenate([other_half, below], axis=0), dc=1)
    other_half, bias_other = got[:own_rows], got[own_rows : own_rows + 1]
    other_state = got[own_rows + 1 : own_rows + 1 + own_state.shape[0]]
    all_state = by_core(*(a.reshape(Z, X, 4, count) for a in (own_state, other_state)), 3, c)
    all_state = turn(turn(all_state, z, 0), x, 1) * (1.0 / STATE_SCALE)
    bias_state = all_state.transpose(2, 1, 0, 3, 4).reshape(4, width)

    def in_order(own, other):
        first, last = jnp.where(c == 0, own, other), jnp.where(c == 0, other, own)
        return jnp.concatenate([first, last], axis=1)

    weight_grad = in_order(own_half, other_half)
    bias_grad = in_order(bias_half, bias_other)[0]

    squared = all_sum(sums[0] + sums[1], ("core", "x", "z"))
    bias_squared = jnp.sum(bias_grad * bias_grad)
    squared, bias_squared, weight_grad, bias_grad, bias_state = lax.optimization_barrier(
        (squared, bias_squared, weight_grad, bias_grad, bias_state)
    )
    sq_norm = jnp.sum(all_sum(squared, ("y",))) + bias_squared
    total_count = width * (own_rows * X * Z * C * Y + 1)
    clip_factor = jnp.minimum(1.0, jnp.sqrt(jnp.float32(total_count)) / jnp.sqrt(sq_norm + 1e-06))
    master_w, moment_w, second_w, teacher_w = adamw_update(
        weight_grad,
        master_weight,
        moment_weight,
        second_weight,
        teacher_weight,
        clip_factor,
        decay_rate,
    )
    own_bias = adamw_update(
        lax.dynamic_slice(bias_grad, (index * count,), (count,)),
        master_bias,
        moment_bias,
        second_bias,
        teacher_bias,
        clip_factor,
        0.0,
    )
    full_bias = adamw_update(bias_grad, *bias_state, clip_factor, 0.0)[3].astype(jnp.bfloat16)
    teacher_half = teacher_w.astype(jnp.bfloat16)
    full_weight = gather_plane(teacher_half, x, z, c)
    return (master_w, moment_w, second_w, teacher_w, *own_bias, full_weight, full_bias)


def solution(mesh):
    placed = (
        P("dp", "mp"),
        P("dp", None),
        P(("mp", "dp"), None),
        P(("mp", "dp"), None),
        P(("mp", "dp"), None),
        P(("mp", "dp"), None),
        P("dp"),
        P("dp"),
        P("dp"),
        P("dp"),
    )
    return jax.shard_map(
        per_device,
        mesh=mesh,
        in_specs=placed,
        out_specs=(
            P(("mp", "dp"), None),
            P(("mp", "dp"), None),
            P(("mp", "dp"), None),
            P(("mp", "dp"), None),
            P("dp"),
            P("dp"),
            P("dp"),
            P("dp"),
            P("mp", None),
            P(),
        ),
        check_vma=False,
    )
```

```python
import functools
import jax
import jax.numpy as jnp
from jax import lax
from jax.experimental import pallas as pl
from jax.experimental.pallas import tpu as pltpu
from jax.sharding import PartitionSpec as P

beta_one = 0.9
beta_two = 0.95
adam_eps = 1e-08
learn_rate = 0.1
decay_rate = 0.05
ema_keep = 0.9
X, Z, C, Y = 4, 4, 2, 4


def adamw_update(gradient, master, moment, second, teacher, clip_factor, decay):
    clipped = clip_factor * gradient
    new_moment = beta_one * moment + (1.0 - beta_one) * clipped
    new_second = beta_two * second + (1.0 - beta_two) * clipped * clipped
    new_master = master - learn_rate * (
        new_moment / (jnp.sqrt(new_second) + adam_eps) + decay * master
    )
    new_teacher = ema_keep * teacher + (1.0 - ema_keep) * new_master
    return (new_master, new_moment, new_second, new_teacher)


NOTE = 8
STATE_SCALE = 2.0**14


def product_kernel(x_first, side, own, other, own_cols, other_cols, extra, out):
    dims = (((0,), (0,)), ((), ()))
    value = lax.dot_general(own[...], own_cols[...], dims, preferred_element_type=jnp.float32)
    value += lax.dot_general(other[...], other_cols[...], dims, preferred_element_type=jnp.float32)
    peak = jnp.max(jnp.abs(value), axis=0, keepdims=True)
    power = jnp.ceil(jnp.log2(jnp.maximum(peak, 1e-30))) + 1.0
    value = value * jnp.exp2(15.0 - power)
    rows, cols = value.shape
    bias = sum(jnp.sum(r[...].astype(jnp.float32), axis=0, keepdims=True) for r in (own_cols, other_cols))
    bias_power = jnp.ceil(jnp.log2(jnp.maximum(jnp.abs(bias), 1e-30))) + 1.0
    rest = bias * jnp.exp2(15.0 - bias_power)
    lines = [power]
    for _ in range(2):
        piece = rest.astype(jnp.bfloat16).astype(jnp.float32)
        lines.append(piece)
        rest = rest - piece
    lines += [rest, bias_power]
    row = lax.broadcasted_iota(jnp.int32, (NOTE, cols), 0)
    note = extra[...]
    for at, line in enumerate(lines):
        note = jnp.where(row == at, line, note)
    block = rows // X
    small = block // Z
    for i in range(X):
        if x_first:
            out[i, :block, :] = value[i * block : (i + 1) * block]
        else:
            for j in range(X):
                at = j * block + i * small
                out[i, j * small : (j + 1) * small, :] = value[at : at + small]
        out[i, block:, :] = note


def chip_product(attn_own, attn_other, cotangent, start, other_cols, extra, x_first):
    tokens, rows = attn_own.shape
    cols = other_cols.shape[1]
    step = 512
    whole = pl.BlockSpec((tokens, rows), lambda n, side: (0, 0))
    shape = (X, rows // X + NOTE, cols)
    return pl.pallas_call(
        functools.partial(product_kernel, x_first),
        grid_spec=pltpu.PrefetchScalarGridSpec(
            num_scalar_prefetch=1,
            grid=(cols // step,),
            in_specs=[
                whole,
                whole,
                pl.BlockSpec((tokens, step), lambda n, side: (0, side[0] + n)),
                pl.BlockSpec((tokens, step), lambda n, side: (0, n)),
                pl.BlockSpec((NOTE, step), lambda n, side: (0, n)),
            ],
            out_specs=pl.BlockSpec((*shape[:2], step), lambda n, side: (0, 0, n)),
        ),
        out_shape=jax.ShapeDtypeStruct(shape, jnp.float32),
        compiler_params=pltpu.CompilerParams(
            dimension_semantics=("arbitrary",), vmem_limit_bytes=40 * 2**20
        ),
        cost_estimate=pl.CostEstimate(flops=1, bytes_accessed=1, transcendentals=0),
    )((start // step).reshape(1).astype(jnp.int32), attn_own, attn_other, cotangent, other_cols, extra)


def place(x, z, c):
    return (x % X) * (Z * C) + (z % Z) * C + c % C


def shift(array, dx=0, dz=0, dc=0):
    pairs = [
        (place(x, z, c), place(x + dx, z + dz, c + dc))
        for x in range(X)
        for z in range(Z)
        for c in range(C)
    ]
    return lax.ppermute(array, "dp", pairs)


def shift_y(array, dy):
    return lax.ppermute(array, "mp", [(y, (y + dy) % Y) for y in range(Y)])


def along_x(array, d):
    return shift(array, dx=d)


def along_z(array, d):
    return shift(array, dz=d)


def all_sum(array, ways):
    for way in ways:
        if way == "core":
            array = array + shift(array, dc=1)
        else:
            move = {"x": along_x, "z": along_z, "y": shift_y}[way]
            array = array + move(array, 1) + move(array, 2) + move(array, 3)
    return array


def pick(array, axis, index):
    return lax.dynamic_index_in_dim(array, index % array.shape[axis], axis, keepdims=False)


def turn(array, me, axis):
    back = jnp.flip(array, axis)
    size = array.shape[axis]
    twice = jnp.concatenate([back, lax.slice_in_dim(back, 0, size - 1, axis=axis)], axis=axis)
    return lax.dynamic_slice_in_dim(twice, size - 1 - me, size, axis=axis)


def scatter_sum(blocks, me, rows, move):
    own = pick(blocks, 0, me)
    total, rest = own[:rows], {0: own[rows:]}
    far = (2, 1, 3)
    parts = lax.optimization_barrier([move(pick(blocks, 0, me + d), d) for d in far])
    for d, got in zip(far, parts):
        total, rest[d] = total + got[:rows], got[rows:]
    return total, [rest[d] for d in range(4)]


def coded_pieces(blocks, me):
    return [pick(blocks, 0, me + d).astype(jnp.float16) for d in (2, 1, 3)]


def decoded(piece):
    piece = piece.astype(jnp.float32)
    rows = piece.shape[0] - NOTE
    note = [piece[rows + i : rows + i + 1] for i in range(5)]
    value = piece[:rows] * jnp.exp2(note[0] - 15.0)
    return value, (note[1] + note[2] + note[3]) * jnp.exp2(note[4] - 15.0)


def coded_sum(blocks, pieces, me, move, entries):
    own = pick(blocks, 0, me)
    total, bias = decoded(own)
    noted = {0: own[5 - NOTE :, :entries]}
    for d, piece in zip((2, 1, 3), pieces):
        got = move(piece, d)
        value, line = decoded(got)
        total, bias = total + value, bias + line
        noted[d] = got[5 - NOTE :, :entries].astype(jnp.float32)
    cols = total.shape[1]
    lines = [bias]
    if entries:
        flat = jnp.concatenate([jnp.sum(noted[d], axis=0) for d in range(4)])
        lines.append(jnp.pad(flat, (0, -flat.size % cols)).reshape(-1, cols))
    below = jnp.concatenate(lines, axis=0)
    below = jnp.pad(below, ((0, 8 - below.shape[0]), (0, 0)))
    below = jnp.broadcast_to(below[None], (X, 8, cols))
    return jnp.concatenate([total.reshape(X, -1, cols), below], axis=1)


def gather_line(own, me, move):
    got = [own] + [move(own, d) for d in (1, 2, 3)]
    turned = jnp.stack([got[3], got[2], got[1], got[0], got[3], got[2], got[1]])
    return lax.dynamic_slice_in_dim(turned, 3 - me, 4, axis=0)


def nothing(out):
    pass


def blank(shape, dtype):
    return pl.pallas_call(
        nothing,
        out_shape=jax.ShapeDtypeStruct(shape, dtype),
        out_specs=pl.BlockSpec(memory_space=pl.ANY),
    )()


def by_core(own, twin, axis, c):
    own, twin = jnp.expand_dims(own, axis), jnp.expand_dims(twin, axis)
    shape = [1] * own.ndim
    shape[axis] = C
    return jnp.where(lax.broadcasted_iota(jnp.int32, shape, axis) == c, own, twin)


def gather_plane(rows, x, z, c):
    count, width = rows.shape
    half = width // 2
    full = blank((X, Z, C, count, width), rows.dtype)
    line_a = gather_line(rows[:, :half], z, along_z)
    line_b = gather_line(rows[:, half:], x, along_x)
    line_a, line_b = lax.optimization_barrier((line_a, line_b))
    lines, moves = (line_a, line_b), (along_x, along_z)

    def put(full, which, d, low, part, twin):
        zero, low, start = jnp.int32(0), jnp.int32(low), jnp.int32(which * half)
        piece = by_core(part, twin, 1, c)
        if which == 0:
            piece, at = piece[None], ((x - d) % X, low, zero, zero, start)
        else:
            piece, at = piece[:, None], (low, (z - d) % Z, zero, zero, start)
        return lax.dynamic_update_slice(full, piece, at)

    near = [(i, d, moves[i](lines[i], d)) for d in (1, -1) for i in (0, 1)]
    for i in (0, 1):
        full = put(full, i, 0, 0, lines[i], shift(lines[i], dc=1))
    near_parts, full = lax.optimization_barrier(([part for _, _, part in near], full))
    far = []
    for (i, d, _), part in zip(near, near_parts):
        low = 0 if d == 1 else 2
        far.append((i, low, moves[i](part[low : low + 2], d)))
    twins = lax.optimization_barrier([shift(part, dc=1) for part in near_parts])
    for (i, d, _), part, twin in zip(near, near_parts, twins):
        full = put(full, i, d, 0, part, twin)
    far_parts, full = lax.optimization_barrier(([part for _, _, part in far], full))
    for (i, low, _), part in zip(far, far_parts):
        full = put(full, i, 2, low, part, shift(part, dc=1))
    return full.reshape(X * Z * C * count, width)


def squares(array):
    rows, cols = array.shape
    return jnp.sum((array * array).reshape(rows // 8, 8, cols // 128, 128), axis=(0, 2))


def per_device(
    attn_out,
    cotangent,
    master_weight,
    moment_weight,
    second_weight,
    teacher_weight,
    master_bias,
    moment_bias,
    second_bias,
    teacher_bias,
):
    index = lax.axis_index("dp")
    x, z, c = index // (Z * C), (index // C) % Z, index % C
    width = cotangent.shape[1]
    half = width // 2
    sizes = (half * 1536 // 3072, half * 1536 // 3072)
    tokens = cotangent.shape[0]
    own_rows = master_weight.shape[0]

    def columns(array, which):
        start = (1 - c) * half + which * sizes[0]
        return lax.dynamic_slice(array, (0, start), (tokens, sizes[which]))

    attn_other = shift(attn_out, dc=1)
    sent = [columns(cotangent, 0)]
    held, sent[0] = lax.optimization_barrier((cotangent, sent[0]))
    sent.append(columns(held, 1))
    others = [shift(part, dc=1) for part in sent]
    count = master_bias.shape[0]
    rest = jnp.concatenate([master_bias, moment_bias, second_bias, teacher_bias])[None] * STATE_SCALE
    state = []
    for _ in range(2):
        state.append(lax.reduce_precision(rest, 8, 7))
        rest = rest - state[-1]
    state = jnp.concatenate([*state, rest], axis=0)
    entries = state.shape[1]
    extras = [
        jnp.pad(state, ((NOTE - 3, 0), (0, sizes[0] - entries))),
        jnp.zeros((NOTE, sizes[1]), jnp.float32),
    ]

    def blocks_of(which):
        start = c * half + which * sizes[0]
        return chip_product(attn_out, attn_other, cotangent, start, others[which], extras[which], which == 0)

    blocks_a = blocks_of(0)
    pieces_a = coded_pieces(blocks_a, x)
    others[1], pieces_a = lax.optimization_barrier((others[1], pieces_a))
    blocks_b = blocks_of(1)
    pieces_b = coded_pieces(blocks_b, z)
    part_a = coded_sum(blocks_a, pieces_a, x, along_x, entries)
    part_b = coded_sum(blocks_b, pieces_b, z, along_z, 0)
    rows = own_rows * C
    grad_a, noted = scatter_sum(part_a, z, rows + 1, along_z)
    grad_b, _ = scatter_sum(part_b, x, rows + 1, along_x)
    grads = [grad_a, grad_b]
    own_state = jnp.stack([n.reshape(-1)[: X * entries] for n in noted]).reshape(-1, half)
    sums = [squares(g[:rows]) for g in grads]
    bias_half = jnp.concatenate([g[rows : rows + 1] for g in grads], axis=1)
    chip_grad = jnp.concatenate([g[:rows] for g in grads], axis=1).reshape(C, own_rows, half)
    own_half = pick(chip_grad, 0, c)
    other_half = pick(chip_grad, 0, 1 - c)
    below = jnp.concatenate([bias_half, own_state], axis=0)
    below = jnp.pad(below, ((0, -below.shape[0] % 8), (0, 0)))
    got = shift(jnp.concatenate([other_half, below], axis=0), dc=1)
    other_half, bias_other = got[:own_rows], got[own_rows : own_rows + 1]
    other_state = got[own_rows + 1 : own_rows + 1 + own_state.shape[0]]
    all_state = by_core(*(a.reshape(Z, X, 4, count) for a in (own_state, other_state)), 3, c)
    all_state = turn(turn(all_state, z, 0), x, 1) * (1.0 / STATE_SCALE)
    bias_state = all_state.transpose(2, 1, 0, 3, 4).reshape(4, width)

    def in_order(own, other):
        first, last = jnp.where(c == 0, own, other), jnp.where(c == 0, other, own)
        return jnp.concatenate([first, last], axis=1)

    weight_grad = in_order(own_half, other_half)
    bias_grad = in_order(bias_half, bias_other)[0]

    squared = all_sum(sums[0] + sums[1], ("core", "x", "z"))
    bias_squared = jnp.sum(bias_grad * bias_grad)
    squared, bias_squared, weight_grad, bias_grad, bias_state = lax.optimization_barrier(
        (squared, bias_squared, weight_grad, bias_grad, bias_state)
    )
    sq_norm = jnp.sum(all_sum(squared, ("y",))) + bias_squared
    total_count = width * (own_rows * X * Z * C * Y + 1)
    clip_factor = jnp.minimum(1.0, jnp.sqrt(jnp.float32(total_count)) / jnp.sqrt(sq_norm + 1e-06))
    master_w, moment_w, second_w, teacher_w = adamw_update(
        weight_grad,
        master_weight,
        moment_weight,
        second_weight,
        teacher_weight,
        clip_factor,
        decay_rate,
    )
    own_bias = adamw_update(
        lax.dynamic_slice(bias_grad, (index * count,), (count,)),
        master_bias,
        moment_bias,
        second_bias,
        teacher_bias,
        clip_factor,
        0.0,
    )
    full_bias = adamw_update(bias_grad, *bias_state, clip_factor, 0.0)[3].astype(jnp.bfloat16)
    teacher_half = teacher_w.astype(jnp.bfloat16)
    full_weight = gather_plane(teacher_half, x, z, c)
    return (master_w, moment_w, second_w, teacher_w, *own_bias, full_weight, full_bias)


def solution(mesh):
    placed = (
        P("dp", "mp"),
        P("dp", None),
        P(("mp", "dp"), None),
        P(("mp", "dp"), None),
        P(("mp", "dp"), None),
        P(("mp", "dp"), None),
        P("dp"),
        P("dp"),
        P("dp"),
        P("dp"),
    )
    return jax.shard_map(
        per_device,
        mesh=mesh,
        in_specs=placed,
        out_specs=(
            P(("mp", "dp"), None),
            P(("mp", "dp"), None),
            P(("mp", "dp"), None),
            P(("mp", "dp"), None),
            P("dp"),
            P("dp"),
            P("dp"),
            P("dp"),
            P("mp", None),
            P(),
        ),
        check_vma=False,
    )
```

```python
import functools
import jax
import jax.numpy as jnp
from jax import lax
from jax.experimental import pallas as pl
from jax.experimental.pallas import tpu as pltpu
from jax.sharding import PartitionSpec as P

beta_one = 0.9
beta_two = 0.95
adam_eps = 1e-08
learn_rate = 0.1
decay_rate = 0.05
ema_keep = 0.9
X, Z, C, Y = 4, 4, 2, 4


def adamw_update(gradient, master, moment, second, teacher, clip_factor, decay):
    clipped = clip_factor * gradient
    new_moment = beta_one * moment + (1.0 - beta_one) * clipped
    new_second = beta_two * second + (1.0 - beta_two) * clipped * clipped
    new_master = master - learn_rate * (
        new_moment / (jnp.sqrt(new_second) + adam_eps) + decay * master
    )
    new_teacher = ema_keep * teacher + (1.0 - ema_keep) * new_master
    return (new_master, new_moment, new_second, new_teacher)


NOTE = 8
STATE_SCALE = 2.0**14


def product_kernel(x_first, side, own, other, own_cols, other_cols, extra, out):
    dims = (((0,), (0,)), ((), ()))
    value = lax.dot_general(own[...], own_cols[...], dims, preferred_element_type=jnp.float32)
    value += lax.dot_general(other[...], other_cols[...], dims, preferred_element_type=jnp.float32)
    peak = jnp.max(jnp.abs(value), axis=0, keepdims=True)
    power = jnp.ceil(jnp.log2(jnp.maximum(peak, 1e-30))) + 1.0
    value = value * jnp.exp2(15.0 - power)
    rows, cols = value.shape
    bias = sum(jnp.sum(r[...].astype(jnp.float32), axis=0, keepdims=True) for r in (own_cols, other_cols))
    bias_power = jnp.ceil(jnp.log2(jnp.maximum(jnp.abs(bias), 1e-30))) + 1.0
    rest = bias * jnp.exp2(15.0 - bias_power)
    lines = [power]
    for _ in range(2):
        piece = rest.astype(jnp.bfloat16).astype(jnp.float32)
        lines.append(piece)
        rest = rest - piece
    lines += [rest, bias_power]
    row = lax.broadcasted_iota(jnp.int32, (NOTE, cols), 0)
    note = extra[...]
    for at, line in enumerate(lines):
        note = jnp.where(row == at, line, note)
    block = rows // X
    small = block // Z
    for i in range(X):
        if x_first:
            out[i, :block, :] = value[i * block : (i + 1) * block]
        else:
            for j in range(X):
                at = j * block + i * small
                out[i, j * small : (j + 1) * small, :] = value[at : at + small]
        out[i, block:, :] = note


def chip_product(attn_own, attn_other, cotangent, start, other_cols, extra, x_first):
    tokens, rows = attn_own.shape
    cols = other_cols.shape[1]
    step = 512
    whole = pl.BlockSpec((tokens, rows), lambda n, side: (0, 0))
    shape = (X, rows // X + NOTE, cols)
    return pl.pallas_call(
        functools.partial(product_kernel, x_first),
        grid_spec=pltpu.PrefetchScalarGridSpec(
            num_scalar_prefetch=1,
            grid=(cols // step,),
            in_specs=[
                whole,
                whole,
                pl.BlockSpec((tokens, step), lambda n, side: (0, side[0] + n)),
                pl.BlockSpec((tokens, step), lambda n, side: (0, n)),
                pl.BlockSpec((NOTE, step), lambda n, side: (0, n)),
            ],
            out_specs=pl.BlockSpec((*shape[:2], step), lambda n, side: (0, 0, n)),
        ),
        out_shape=jax.ShapeDtypeStruct(shape, jnp.float32),
        compiler_params=pltpu.CompilerParams(
            dimension_semantics=("arbitrary",), vmem_limit_bytes=40 * 2**20
        ),
        cost_estimate=pl.CostEstimate(flops=1, bytes_accessed=1, transcendentals=0),
    )((start // step).reshape(1).astype(jnp.int32), attn_own, attn_other, cotangent, other_cols, extra)


def place(x, z, c):
    return (x % X) * (Z * C) + (z % Z) * C + c % C


def shift(array, dx=0, dz=0, dc=0):
    pairs = [
        (place(x, z, c), place(x + dx, z + dz, c + dc))
        for x in range(X)
        for z in range(Z)
        for c in range(C)
    ]
    return lax.ppermute(array, "dp", pairs)


def shift_y(array, dy):
    return lax.ppermute(array, "mp", [(y, (y + dy) % Y) for y in range(Y)])


def along_x(array, d):
    return shift(array, dx=d)


def along_z(array, d):
    return shift(array, dz=d)


def all_sum(array, ways):
    for way in ways:
        if way == "core":
            array = array + shift(array, dc=1)
        else:
            move = {"x": along_x, "z": along_z, "y": shift_y}[way]
            parts = lax.optimization_barrier([move(array, d) for d in (2, 1, 3)])
            array = array + parts[0] + parts[1] + parts[2]
    return array


def pick(array, axis, index):
    return lax.dynamic_index_in_dim(array, index % array.shape[axis], axis, keepdims=False)


def turn(array, me, axis):
    back = jnp.flip(array, axis)
    size = array.shape[axis]
    twice = jnp.concatenate([back, lax.slice_in_dim(back, 0, size - 1, axis=axis)], axis=axis)
    return lax.dynamic_slice_in_dim(twice, size - 1 - me, size, axis=axis)


def scatter_sum(blocks, me, rows, move):
    own = pick(blocks, 0, me)
    total, rest = own[:rows], {0: own[rows:]}
    far = (2, 1, 3)
    parts = lax.optimization_barrier([move(pick(blocks, 0, me + d), d) for d in far])
    for d, got in zip(far, parts):
        total, rest[d] = total + got[:rows], got[rows:]
    return total, [rest[d] for d in range(4)]


def coded_pieces(blocks, me):
    return [pick(blocks, 0, me + d).astype(jnp.float16) for d in (2, 1, 3)]


def decoded(piece):
    piece = piece.astype(jnp.float32)
    rows = piece.shape[0] - NOTE
    note = [piece[rows + i : rows + i + 1] for i in range(5)]
    value = piece[:rows] * jnp.exp2(note[0] - 15.0)
    return value, (note[1] + note[2] + note[3]) * jnp.exp2(note[4] - 15.0)


def coded_sum(blocks, pieces, me, move, entries):
    own = pick(blocks, 0, me)
    total, bias = decoded(own)
    noted = {0: own[5 - NOTE :, :entries]}
    for d, piece in zip((2, 1, 3), pieces):
        got = move(piece, d)
        value, line = decoded(got)
        total, bias = total + value, bias + line
        noted[d] = got[5 - NOTE :, :entries].astype(jnp.float32)
    cols = total.shape[1]
    lines = [bias]
    if entries:
        flat = jnp.concatenate([jnp.sum(noted[d], axis=0) for d in range(4)])
        lines.append(jnp.pad(flat, (0, -flat.size % cols)).reshape(-1, cols))
    below = jnp.concatenate(lines, axis=0)
    below = jnp.pad(below, ((0, 8 - below.shape[0]), (0, 0)))
    below = jnp.broadcast_to(below[None], (X, 8, cols))
    return jnp.concatenate([total.reshape(X, -1, cols), below], axis=1)


def gather_line(own, me, move):
    got = [own, *lax.optimization_barrier([move(own, d) for d in (1, 2, 3)])]
    turned = jnp.stack([got[3], got[2], got[1], got[0], got[3], got[2], got[1]])
    return lax.dynamic_slice_in_dim(turned, 3 - me, 4, axis=0)


def nothing(out):
    pass


def blank(shape, dtype):
    return pl.pallas_call(
        nothing,
        out_shape=jax.ShapeDtypeStruct(shape, dtype),
        out_specs=pl.BlockSpec(memory_space=pl.ANY),
    )()


def by_core(own, twin, axis, c):
    own, twin = jnp.expand_dims(own, axis), jnp.expand_dims(twin, axis)
    shape = [1] * own.ndim
    shape[axis] = C
    return jnp.where(lax.broadcasted_iota(jnp.int32, shape, axis) == c, own, twin)


def gather_plane(rows, x, z, c):
    count, width = rows.shape
    half = width // 2
    full = blank((X, Z, C, count, width), rows.dtype)
    line_a = gather_line(rows[:, :half], z, along_z)
    line_b = gather_line(rows[:, half:], x, along_x)
    line_a, line_b = lax.optimization_barrier((line_a, line_b))
    lines, moves = (line_a, line_b), (along_x, along_z)

    def put(full, which, d, low, part, twin):
        zero, low, start = jnp.int32(0), jnp.int32(low), jnp.int32(which * half)
        piece = by_core(part, twin, 1, c)
        if which == 0:
            piece, at = piece[None], ((x - d) % X, low, zero, zero, start)
        else:
            piece, at = piece[:, None], (low, (z - d) % Z, zero, zero, start)
        return lax.dynamic_update_slice(full, piece, at)

    near = [(i, d, moves[i](lines[i], d)) for d in (1, -1) for i in (0, 1)]
    for i in (0, 1):
        full = put(full, i, 0, 0, lines[i], shift(lines[i], dc=1))
    near_parts, full = lax.optimization_barrier(([part for _, _, part in near], full))
    far = []
    for (i, d, _), part in zip(near, near_parts):
        low = 0 if d == 1 else 2
        far.append((i, low, moves[i](part[low : low + 2], d)))
    twins = lax.optimization_barrier([shift(part, dc=1) for part in near_parts])
    for (i, d, _), part, twin in zip(near, near_parts, twins):
        full = put(full, i, d, 0, part, twin)
    far_parts, full = lax.optimization_barrier(([part for _, _, part in far], full))
    for (i, low, _), part in zip(far, far_parts):
        full = put(full, i, 2, low, part, shift(part, dc=1))
    return full.reshape(X * Z * C * count, width)


def squares(array):
    rows, cols = array.shape
    return jnp.sum((array * array).reshape(rows // 8, 8, cols // 128, 128), axis=(0, 2))


def per_device(
    attn_out,
    cotangent,
    master_weight,
    moment_weight,
    second_weight,
    teacher_weight,
    master_bias,
    moment_bias,
    second_bias,
    teacher_bias,
):
    index = lax.axis_index("dp")
    x, z, c = index // (Z * C), (index // C) % Z, index % C
    width = cotangent.shape[1]
    half = width // 2
    sizes = (half * 1536 // 3072, half * 1536 // 3072)
    tokens = cotangent.shape[0]
    own_rows = master_weight.shape[0]

    def columns(array, which):
        start = (1 - c) * half + which * sizes[0]
        return lax.dynamic_slice(array, (0, start), (tokens, sizes[which]))

    attn_other = shift(attn_out, dc=1)
    sent = [columns(cotangent, 0)]
    held, sent[0] = lax.optimization_barrier((cotangent, sent[0]))
    sent.append(columns(held, 1))
    others = [shift(part, dc=1) for part in sent]
    count = master_bias.shape[0]
    rest = jnp.concatenate([master_bias, moment_bias, second_bias, teacher_bias])[None] * STATE_SCALE
    state = []
    for _ in range(2):
        state.append(lax.reduce_precision(rest, 8, 7))
        rest = rest - state[-1]
    state = jnp.concatenate([*state, rest], axis=0)
    entries = state.shape[1]
    extras = [
        jnp.pad(state, ((NOTE - 3, 0), (0, sizes[0] - entries))),
        jnp.zeros((NOTE, sizes[1]), jnp.float32),
    ]

    def blocks_of(which):
        start = c * half + which * sizes[0]
        return chip_product(attn_out, attn_other, cotangent, start, others[which], extras[which], which == 0)

    blocks_a = blocks_of(0)
    pieces_a = coded_pieces(blocks_a, x)
    others[1], pieces_a = lax.optimization_barrier((others[1], pieces_a))
    blocks_b = blocks_of(1)
    pieces_b = coded_pieces(blocks_b, z)
    part_a = coded_sum(blocks_a, pieces_a, x, along_x, entries)
    part_b = coded_sum(blocks_b, pieces_b, z, along_z, 0)
    rows = own_rows * C
    grad_a, noted = scatter_sum(part_a, z, rows + 1, along_z)
    grad_b, _ = scatter_sum(part_b, x, rows + 1, along_x)
    grads = [grad_a, grad_b]
    own_state = jnp.stack([n.reshape(-1)[: X * entries] for n in noted]).reshape(-1, half)
    sums = [squares(g[:rows]) for g in grads]
    bias_half = jnp.concatenate([g[rows : rows + 1] for g in grads], axis=1)
    chip_grad = jnp.concatenate([g[:rows] for g in grads], axis=1).reshape(C, own_rows, half)
    own_half = pick(chip_grad, 0, c)
    other_half = pick(chip_grad, 0, 1 - c)
    below = jnp.concatenate([bias_half, own_state], axis=0)
    below = jnp.pad(below, ((0, -below.shape[0] % 8), (0, 0)))
    got = shift(jnp.concatenate([other_half, below], axis=0), dc=1)
    other_half, bias_other = got[:own_rows], got[own_rows : own_rows + 1]
    other_state = got[own_rows + 1 : own_rows + 1 + own_state.shape[0]]
    all_state = by_core(*(a.reshape(Z, X, 4, count) for a in (own_state, other_state)), 3, c)
    all_state = turn(turn(all_state, z, 0), x, 1) * (1.0 / STATE_SCALE)
    bias_state = all_state.transpose(2, 1, 0, 3, 4).reshape(4, width)

    def in_order(own, other):
        first, last = jnp.where(c == 0, own, other), jnp.where(c == 0, other, own)
        return jnp.concatenate([first, last], axis=1)

    weight_grad = in_order(own_half, other_half)
    bias_grad = in_order(bias_half, bias_other)[0]

    squared = all_sum(sums[0] + sums[1], ("core", "x", "z"))
    bias_squared = jnp.sum(bias_grad * bias_grad)
    squared, bias_squared, weight_grad, bias_grad, bias_state = lax.optimization_barrier(
        (squared, bias_squared, weight_grad, bias_grad, bias_state)
    )
    sq_norm = jnp.sum(all_sum(squared, ("y",))) + bias_squared
    total_count = width * (own_rows * X * Z * C * Y + 1)
    clip_factor = jnp.minimum(1.0, jnp.sqrt(jnp.float32(total_count)) / jnp.sqrt(sq_norm + 1e-06))
    master_w, moment_w, second_w, teacher_w = adamw_update(
        weight_grad,
        master_weight,
        moment_weight,
        second_weight,
        teacher_weight,
        clip_factor,
        decay_rate,
    )
    own_bias = adamw_update(
        lax.dynamic_slice(bias_grad, (index * count,), (count,)),
        master_bias,
        moment_bias,
        second_bias,
        teacher_bias,
        clip_factor,
        0.0,
    )
    full_bias = adamw_update(bias_grad, *bias_state, clip_factor, 0.0)[3].astype(jnp.bfloat16)
    teacher_half = teacher_w.astype(jnp.bfloat16)
    full_weight = gather_plane(teacher_half, x, z, c)
    return (master_w, moment_w, second_w, teacher_w, *own_bias, full_weight, full_bias)


def solution(mesh):
    placed = (
        P("dp", "mp"),
        P("dp", None),
        P(("mp", "dp"), None),
        P(("mp", "dp"), None),
        P(("mp", "dp"), None),
        P(("mp", "dp"), None),
        P("dp"),
        P("dp"),
        P("dp"),
        P("dp"),
    )
    return jax.shard_map(
        per_device,
        mesh=mesh,
        in_specs=placed,
        out_specs=(
            P(("mp", "dp"), None),
            P(("mp", "dp"), None),
            P(("mp", "dp"), None),
            P(("mp", "dp"), None),
            P("dp"),
            P("dp"),
            P("dp"),
            P("dp"),
            P("mp", None),
            P(),
        ),
        check_vma=False,
    )
```
